32 devices in a mesh: radial: 4 (over y, core), lateral: 8 (over z, x).
Axes of the slice: x: 2, y: 2, z: 4, core: 2. Of those that a mesh axis runs over, the one named last changes fastest.
Arguments:
- pressure: float32 [128, 32, 512], P('radial', 'lateral'), may hold values from -6 to 6
- residual: float32 [128, 32, 512], P('radial', 'lateral'), may hold values from -45 to 45
- inv_visc: float32 [128, 32, 512], P('radial', 'lateral'), may hold values from 0.1 to 10
- thermal: float32 [128, 32, 512], P('radial', 'lateral'), may hold values from -6 to 6
- compress: float32 [128], P('radial'), may hold values from 0.3 to 3
- legendre: bfloat16 [32, 256, 256], P('lateral'), may hold values from -1.5 to 1.5
- kernels: float32 [2, 128, 256], P(None, 'radial'), may hold values from -0.5 to 0.5
Outputs:
- pressure_new: float32 [128, 32, 512], P('radial', 'lateral')
- residual_new: float32 [128, 32, 512], P('radial', 'lateral')
- geoid_coef: float32 [256, 2, 256], P('lateral')
- topo_coef: float32 [256, 2, 256], P('lateral')
The draws below stay inside these ranges and needn't reach their ends.
All inputs are finite; a program needn't handle non-finite values.
Results may differ from the reference program's by a relative error of at most 0.0051.
Values may be sent and summed in bfloat16 or wider, within the bound.
A program may use at most 128 MiB of HBM per device.

```python
import math
import jax
import jax.numpy as jnp
from jax import lax

LDEG = 256
MORD = 256
NLON = 512
SHELLS = 128
NLAT = 32


def draw_residual(key, part):
    key_base = jax.random.fold_in(key, 11)
    key_rough = jax.random.fold_in(key, 12)
    shell = jnp.arange(SHELLS, dtype=jnp.float32)[:, None, None]
    cycle = jnp.arange(NLAT, dtype=jnp.float32)[None, :, None]
    trend = (1.0 + 2.0 * cycle / max(NLAT - 1, 1)) * (1.0 + shell / max(SHELLS - 1, 1))
    rough = 10.0 ** jax.random.uniform(key_rough, (SHELLS, NLAT, 1), jnp.float32, -0.5, 0.5)
    base = jax.random.truncated_normal(key_base, -4.0, 4.0, (SHELLS, NLAT, NLON), jnp.float32)
    return 0.5 * base * rough * trend


def strengthened(array, rng, source, target, shards_of, factor):
    def block_of(position):
        return (jnp.arange(array.shape[position]) // (array.shape[position] // shards_of)).reshape((-1,) + (1,) * (array.ndim - 1 - position))

    one_side = jax.random.permutation(rng, shards_of)[block_of(target)]
    other_side = (block_of(target) + shards_of // 2) % shards_of
    return jnp.where((block_of(source) == one_side) | (block_of(source) == other_side), factor * array, array)


def level_of(own_key, dims, pieces, smallest, high):
    gain, own = 1.0, jax.random.fold_in(own_key, 6)
    for position, parts in pieces:
        draws = jnp.exp(jax.random.uniform(jax.random.fold_in(own, position), (parts,), jnp.float32, smallest / len(pieces), high / len(pieces)))
        gain = gain * jnp.repeat(draws, dims[position] // parts).reshape([-1 if axis == position else 1 for axis in range(len(dims))])
    return gain


def bell_draw(own_key, shape, deviation, reach, split=(), kind=jnp.bfloat16):
    loudness = level_of(own_key, shape, split, -0.22, 0.18) if split else 1.0
    array = jax.random.normal(own_key, shape, jnp.float32) * deviation * loudness
    return jnp.minimum(jnp.maximum(array, -reach), reach).astype(kind)


def bell_draw_with(own_key, shape, spread, reach, cuts, heavy, held_as=jnp.bfloat16):
    drawn = spread * jax.random.normal(own_key, shape, jnp.float32)
    if cuts:
        drawn = drawn * level_of(own_key, shape, cuts, -0.22, 0.18)
    return jnp.clip(strengthened(drawn, jax.random.fold_in(own_key, 3), *heavy), -reach, reach).astype(held_as)


def setup_inputs(seed: int = 0) -> dict:
    arg_keys = jax.random.split(jax.random.key(seed), 8)
    pressure = bell_draw(arg_keys[0], (SHELLS, NLAT, NLON), 1.0, 6.0, ((0, 4), (1, 8)), jnp.float32)
    residual = draw_residual(jax.random.fold_in(arg_keys[7], 71), 0)
    inv_visc = jnp.clip(jnp.exp(math.log(10.0) - 4.6051702 * jax.random.uniform(arg_keys[2], (SHELLS, NLAT, NLON), jnp.float32) ** level_of(arg_keys[2], (SHELLS, NLAT, NLON), ((0, 4), (1, 8)), -0.2, 0.2)), 0.1, 10.0)
    thermal = bell_draw(arg_keys[3], (SHELLS, NLAT, NLON), 1.0, 6.0, ((0, 4), (1, 8)), jnp.float32)
    compress = jnp.clip(jnp.exp(math.log(3.0) - 2.3025851 * jax.random.uniform(arg_keys[4], (SHELLS,), jnp.float32) ** level_of(arg_keys[4], (SHELLS,), ((0, 4),), -0.2, 0.2)), 0.3, 3.0)
    legendre = bell_draw_with(arg_keys[5], (NLAT, LDEG, MORD), NLAT ** -0.5, 1.5, ((0, 8),), (0, 1, 8, 2.0))
    kernels = bell_draw(arg_keys[6], (2, SHELLS, LDEG), SHELLS ** -0.5, 0.5, ((1, 4),), jnp.float32)
    return {"pressure": pressure, "residual": residual, "inv_visc": inv_visc, "thermal": thermal, "compress": compress, "legendre": legendre, "kernels": kernels}


def fourier_table(nlon, orders):
    column = jnp.arange(nlon, dtype=jnp.int32)[:, None]
    order = jnp.arange(orders, dtype=jnp.int32)[None, :]
    phase = 2.0 * math.pi / nlon * (column * order % nlon).astype(jnp.float32)
    scale = 1.0 / math.sqrt(nlon)
    return (jnp.concatenate([jnp.cos(phase), jnp.sin(phase)], axis=1) * scale).astype(jnp.bfloat16)

def reference(pressure, residual, inv_visc, thermal, compress, legendre, kernels):
    padded = jnp.pad(residual, ((1, 1), (1, 1), (0, 0)))
    beside = padded[2:, 1:-1] + padded[:-2, 1:-1] + padded[1:-1, 2:] + padded[1:-1, :-2]
    beside = beside + jnp.roll(residual, 1, axis=2) + jnp.roll(residual, -1, axis=2)
    image = (6.0 + inv_visc) * residual - beside
    alpha = jnp.sum(residual * residual) / jnp.sum(residual * image)
    pressure_new = pressure + alpha * residual
    residual_new = residual - alpha * image
    anomaly = (thermal - compress[:, None, None] * pressure_new).astype(jnp.bfloat16)
    shells, cycles, nlon = anomaly.shape
    orders = legendre.shape[2]
    table = fourier_table(nlon, orders)
    spectrum = jnp.dot(anomaly.reshape(shells * cycles, nlon), table, preferred_element_type=jnp.float32)
    spectrum = spectrum.astype(jnp.bfloat16).reshape(shells, cycles, 2, orders)
    coefficients = jnp.einsum('satm,alm->lstm', spectrum.astype(jnp.float32), legendre.astype(jnp.float32))
    response = jnp.einsum('ksl,lstm->lktm', kernels, coefficients, precision=lax.Precision.HIGHEST)
    return (pressure_new, residual_new, response[:, 0], response[:, 1])
```

```python
import functools
import math

import jax
import jax.numpy as jnp
import numpy as np
from jax import lax
from jax.experimental import pallas as pl
from jax.experimental.pallas import tpu as pltpu
from jax.sharding import PartitionSpec as P

MESH = pl.DeviceIdType.MESH
F32 = jnp.float32
BF16 = jnp.bfloat16


def fourier_table(nlon, orders):
    column = np.arange(nlon, dtype=np.int32)[:, None]
    order = np.arange(orders, dtype=np.int32)[None, :]
    phase = np.float32(2.0 * math.pi / nlon) * (column * order % nlon).astype(np.float32)
    scale = np.float32(1.0 / math.sqrt(nlon))
    return (np.concatenate([np.cos(phase), np.sin(phase)], axis=1) * scale).astype(BF16)


def send(src, dst, send_sem, recv_sem, axis, target):
    copy = pltpu.make_async_remote_copy(
        src_ref=src,
        dst_ref=dst,
        send_sem=send_sem,
        recv_sem=recv_sem,
        device_id={axis: target},
        device_id_type=MESH,
    )
    copy.start()
    return copy


def folded(x):
    rows = x.shape[0] // 8
    cols = x.shape[1] // 128
    total = None
    for i in range(rows):
        for j in range(cols):
            part = x[i * 8 : (i + 1) * 8, j * 128 : (j + 1) * 128]
            total = part if total is None else total + part
    return total


def kernel(
    nr, nl,
    pres, res, visc, therm, comp, leg, ker, table,
    pres_out, res_out, final,
    shell_send, shell_recv, cycle_send, cycle_recv,
    dot_r, dot_l, spec_send, spec_recv, ker_recv, ker_t, part, wire, terms,
    shell_ss, shell_rs, cycle_ss, cycle_rs,
    dotr_ss, dotr_rs, dotl_ss, dotl_rs,
    spec_ss, spec_rs, ker_ss, ker_rs, term_ss, term_rs, fin_ss, fin_rs,
):
    ri, li = lax.axis_index("radial"), lax.axis_index("lateral")
    shells, cycles, nlon = res.shape
    degrees = leg.shape[1]
    orders = leg.shape[2]
    owned = degrees // nl
    block = table.shape[1] // nr

    barrier = pltpu.get_barrier_semaphore()
    for d in range(1, nr):
        pl.semaphore_signal(barrier, inc=1, device_id={"radial": lax.rem(ri + d, nr)}, device_id_type=MESH)
    for d in range(1, nl):
        pl.semaphore_signal(barrier, inc=1, device_id={"lateral": lax.rem(li + d, nl)}, device_id_type=MESH)

    r = [res[:, a, :] for a in range(cycles)]
    for a in range(cycles):
        shell_send[0, a : a + 1, :] = r[a][0:1]
        shell_send[1, a : a + 1, :] = r[a][shells - 1 : shells]
    cycle_send[0] = r[0]
    cycle_send[1] = r[cycles - 1]
    pl.semaphore_wait(barrier, nr - 1 + nl - 1)

    def edge(sender, receiver, ss, rs, slot, axis, target):
        return pltpu.make_async_remote_copy(
            src_ref=sender.at[slot], dst_ref=receiver.at[slot],
            send_sem=ss.at[slot], recv_sem=rs.at[slot],
            device_id={axis: target}, device_id_type=MESH,
        )

    sides = (
        (cycle_send, cycle_recv, cycle_ss, cycle_rs, "lateral", li, nl),
        (shell_send, shell_recv, shell_ss, shell_rs, "radial", ri, nr),
    )
    for sender, receiver, ss, rs, axis, me, n in sides:
        @pl.when(me > 0)
        def _():
            edge(sender, receiver, ss, rs, 0, axis, lax.rem(me + n - 1, n)).start()

        @pl.when(me < n - 1)
        def _():
            edge(sender, receiver, ss, rs, 1, axis, lax.rem(me + 1, n)).start()

    later = []
    ker_copies = []
    for d in range(1, nr):
        ker_copies.append(send(ker, ker_recv.at[d], ker_ss.at[d], ker_rs.at[d], "radial", lax.rem(ri + d, nr)))

    rows = lax.broadcasted_iota(jnp.int32, (shells, shells), 0)
    lanes = lax.broadcasted_iota(jnp.int32, (shells, shells), 1)
    spread = jnp.broadcast_to(comp[...], (shells, shells))
    scale = jnp.sum(jnp.where(rows == lanes, spread, 0.0), axis=1, keepdims=True)
    row = lax.broadcasted_iota(jnp.int32, (shells, nlon), 0)
    squares = None
    for a in range(cycles):
        term = folded(r[a] * r[a])
        squares = term if squares is None else squares + term

    for sender, receiver, ss, rs, axis, me, n in sides:
        @pl.when(me < n - 1)
        def _():
            edge(sender, receiver, ss, rs, 0, axis, lax.rem(me + 1, n)).wait_recv()

        @pl.when(me == n - 1)
        def _():
            receiver[0] = jnp.zeros(receiver.shape[1:], F32)

        @pl.when(me > 0)
        def _():
            edge(sender, receiver, ss, rs, 1, axis, lax.rem(me + n - 1, n)).wait_recv()

        @pl.when(me == 0)
        def _():
            receiver[1] = jnp.zeros(receiver.shape[1:], F32)

    image = []
    curvature = None
    for a in range(cycles):
        x = r[a]
        up = jnp.where(row == shells - 1, shell_recv[0, a : a + 1, :], pltpu.roll(x, shells - 1, 0))
        down = jnp.where(row == 0, shell_recv[1, a : a + 1, :], pltpu.roll(x, 1, 0))
        following = r[a + 1] if a + 1 < cycles else cycle_recv[0]
        preceding = r[a - 1] if a > 0 else cycle_recv[1]
        beside = up + down + following + preceding
        beside = beside + pltpu.roll(x, 1, 1) + pltpu.roll(x, nlon - 1, 1)
        y = (6.0 + visc[:, a, :]) * x - beside
        image.append(y)
        term = folded(x * y)
        curvature = term if curvature is None else curvature + term

    dot_r[0, 0:8] = squares
    dot_r[0, 8:16] = curvature
    copies = [
        send(dot_r.at[0], dot_r.at[d], dotr_ss.at[d], dotr_rs.at[d], "radial", lax.rem(ri + d, nr))
        for d in range(1, nr)
    ]
    later += copies
    ker_recv[0] = ker[...]
    for copy in ker_copies:
        copy.wait_recv()
    later += ker_copies
    for k in range(2):
        whole = jnp.concatenate([ker_recv[d, k] for d in range(nr)], axis=0).T
        high = whole.astype(BF16)
        ker_t[k, :, 0 : nr * shells] = high
        ker_t[k, :, nr * shells :] = (whole - high.astype(F32)).astype(BF16)
    for copy in copies:
        copy.wait_recv()
    total = dot_r[0]
    for d in range(1, nr):
        total = total + dot_r[d]
    dot_l[0] = total
    copies = [
        send(dot_l.at[0], dot_l.at[d], dotl_ss.at[d], dotl_rs.at[d], "lateral", lax.rem(li + d, nl))
        for d in range(1, nl)
    ]
    later += copies
    for copy in copies:
        copy.wait_recv()
    total = dot_l[0]
    for d in range(1, nl):
        total = total + dot_l[d]
    alpha = jnp.sum(total[0:8], keepdims=True) / jnp.sum(total[8:16], keepdims=True)

    anomaly = []
    for a in range(cycles):
        new = pres[:, a, :] + alpha * r[a]
        pres_out[a] = new
        anomaly.append((therm[:, a, :] - scale * new).astype(BF16))
    spectrum = jnp.dot(jnp.concatenate(anomaly, axis=0), table[...], preferred_element_type=F32).astype(BF16)
    for b in range(nr):
        for a in range(cycles):
            spec_send[b, :, a * block : (a + 1) * block] = spectrum[
                a * shells : (a + 1) * shells, b * block : (b + 1) * block
            ]
    copies = []
    for d in range(1, nr):
        target = lax.rem(ri + d, nr)
        copies.append(send(spec_send.at[target], spec_recv.at[d], spec_ss.at[d], spec_rs.at[d], "radial", target))
    later += copies
    spec_recv[0] = spec_send[ri]
    for a in range(cycles):
        res_out[a] = r[a] - alpha * image[a]
    for copy in copies:
        copy.wait_recv()

    stack = jnp.concatenate([spec_recv[d] for d in range(nr)], axis=0)
    stack = jnp.concatenate([stack, stack], axis=0)
    first = pl.multiple_of(lax.rem(ri * block, orders), block)
    for k in range(2):
        weighted = jnp.dot(ker_t[k], stack, preferred_element_type=F32)
        value = None
        for a in range(cycles):
            term = weighted[:, a * block : (a + 1) * block] * leg[a, :, pl.ds(first, block)].astype(F32)
            value = term if value is None else value + term
        for b in range(nl):
            piece = value[b * owned : (b + 1) * owned]
            part[b, k * owned : (k + 1) * owned, :] = piece
            wire[b, k * owned : (k + 1) * owned, :] = piece.astype(wire.dtype)
    copies = []
    for d in range(1, nl):
        target = lax.rem(li + d, nl)
        copies.append(send(wire.at[target], terms.at[d], term_ss.at[d], term_rs.at[d], "lateral", target))
    later += copies
    total = part[li]
    for d in range(1, nl):
        copies[d - 1].wait_recv()
        total = total + terms[d].astype(F32)
    mine = pl.ds(pl.multiple_of(ri * block, block), block)
    for k in range(2):
        final[k, :, mine] = total[k * owned : (k + 1) * owned]
    copies = [
        send(final.at[:, :, mine], final.at[:, :, mine], fin_ss.at[d], fin_rs.at[d], "radial", lax.rem(ri + d, nr))
        for d in range(1, nr)
    ]
    for d in range(1, nr):
        origin = lax.rem(ri + nr - d, nr)
        theirs = pl.ds(pl.multiple_of(origin * block, block), block)
        pltpu.make_async_remote_copy(
            src_ref=final.at[:, :, theirs], dst_ref=final.at[:, :, theirs],
            send_sem=fin_ss.at[d], recv_sem=fin_rs.at[d],
            device_id={"radial": origin}, device_id_type=MESH,
        ).wait_recv()
    for copy in later + copies:
        copy.wait_send()
    for sender, receiver, ss, rs, axis, me, n in sides:
        @pl.when(me > 0)
        def _():
            edge(sender, receiver, ss, rs, 0, axis, lax.rem(me + n - 1, n)).wait_send()

        @pl.when(me < n - 1)
        def _():
            edge(sender, receiver, ss, rs, 1, axis, lax.rem(me + 1, n)).wait_send()


def on_device(pressure, residual, inv_visc, thermal, compress, legendre, kernels):
    nr, nl = lax.axis_size("radial"), lax.axis_size("lateral")
    shells, cycles, nlon = residual.shape
    degrees, orders = legendre.shape[1:]
    owned = degrees // nl
    block = 2 * orders // nr
    wire = BF16 if owned % 16 == 0 else F32
    table = jnp.asarray(fourier_table(nlon, orders))
    dma = pltpu.SemaphoreType.DMA
    vmem = pl.BlockSpec(memory_space=pltpu.VMEM)
    pressure_new, residual_new, response = pl.pallas_call(
        functools.partial(kernel, nr, nl),
        out_shape=(
            jax.ShapeDtypeStruct((cycles, shells, nlon), F32),
            jax.ShapeDtypeStruct((cycles, shells, nlon), F32),
            jax.ShapeDtypeStruct((2, owned, 2 * orders), F32),
        ),
        in_specs=[vmem] * 8,
        out_specs=(vmem,) * 3,
        scratch_shapes=[
            pltpu.VMEM((2, cycles, nlon), F32),
            pltpu.VMEM((2, cycles, nlon), F32),
            pltpu.VMEM((2, shells, nlon), F32),
            pltpu.VMEM((2, shells, nlon), F32),
            pltpu.VMEM((nr, 16, 128), F32),
            pltpu.VMEM((nl, 16, 128), F32),
            pltpu.VMEM((nr, shells, cycles * block), BF16),
            pltpu.VMEM((nr, shells, cycles * block), BF16),
            pltpu.VMEM((nr, 2, shells, degrees), F32),
            pltpu.VMEM((2, degrees, 2 * nr * shells), BF16),
            pltpu.VMEM((nl, 2 * owned, block), F32),
            pltpu.VMEM((nl, 2 * owned, block), wire),
            pltpu.VMEM((nl, 2 * owned, block), wire),
            dma((2,)), dma((2,)), dma((2,)), dma((2,)),
            dma((nr,)), dma((nr,)), dma((nl,)), dma((nl,)),
            dma((nr,)), dma((nr,)), dma((nr,)), dma((nr,)),
            dma((nl,)), dma((nl,)), dma((nr,)), dma((nr,)),
        ],
        compiler_params=pltpu.CompilerParams(
            collective_id=0, has_side_effects=True, vmem_limit_bytes=40 * 2**20
        ),
    )(pressure, residual, inv_visc, thermal, compress[None, :], legendre, kernels, table)
    response = response.reshape(2, owned, 2, orders)
    return (
        jnp.transpose(pressure_new, (1, 0, 2)),
        jnp.transpose(residual_new, (1, 0, 2)),
        response[0],
        response[1],
    )


def solution(mesh):
    return jax.shard_map(
        on_device,
        mesh=mesh,
        in_specs=(
            P("radial", "lateral", None),
            P("radial", "lateral", None),
            P("radial", "lateral", None),
            P("radial", "lateral", None),
            P("radial"),
            P("lateral", None, None),
            P(None, "radial", None),
        ),
        out_specs=(
            P("radial", "lateral", None),
            P("radial", "lateral", None),
            P("lateral", None, None),
            P("lateral", None, None),
        ),
        check_vma=False,
    )
```

```python
import functools
import math

import jax
import jax.numpy as jnp
import numpy as np
from jax import lax
from jax.experimental import pallas as pl
from jax.experimental.pallas import tpu as pltpu
from jax.sharding import PartitionSpec as P

MESH = pl.DeviceIdType.MESH
F32 = jnp.float32
BF16 = jnp.bfloat16


def fourier_table(nlon, orders):
    column = np.arange(nlon, dtype=np.int32)[:, None]
    order = np.arange(orders, dtype=np.int32)[None, :]
    phase = np.float32(2.0 * math.pi / nlon) * (column * order % nlon).astype(np.float32)
    scale = np.float32(1.0 / math.sqrt(nlon))
    return (np.concatenate([np.cos(phase), np.sin(phase)], axis=1) * scale).astype(BF16)


def send(src, dst, send_sem, recv_sem, axis, target):
    copy = pltpu.make_async_remote_copy(
        src_ref=src,
        dst_ref=dst,
        send_sem=send_sem,
        recv_sem=recv_sem,
        device_id={axis: target},
        device_id_type=MESH,
    )
    copy.start()
    return copy


def folded(x):
    rows = x.shape[0] // 8
    cols = x.shape[1] // 128
    total = None
    for i in range(rows):
        for j in range(cols):
            part = x[i * 8 : (i + 1) * 8, j * 128 : (j + 1) * 128]
            total = part if total is None else total + part
    return total


def kernel(
    nr, nl,
    pres_hbm, res_hbm, visc_hbm, therm_hbm, comp_hbm, leg_hbm, ker_hbm, table_hbm,
    pres_hbm_out, res_hbm_out, geoid_hbm_out, topo_hbm_out,
    pres, res, visc, therm, comp, leg, ker, table, load_sem, final,
    pres_out, res_out, geoid_out, topo_out, store_sem,
    shell_send, shell_recv, cycle_send, cycle_recv,
    dot_r, dot_l, spec_send, spec_recv, ker_recv, ker_t, part, wire, terms,
    shell_ss, shell_rs, cycle_ss, cycle_rs,
    dotr_ss, dotr_rs, dotl_ss, dotl_rs,
    spec_ss, spec_rs, ker_ss, ker_rs, term_ss, term_rs, fin_ss, fin_rs,
):
    ri, li = lax.axis_index("radial"), lax.axis_index("lateral")
    shells, cycles, nlon = res.shape
    degrees = leg.shape[1]
    orders = leg.shape[2]
    owned = degrees // nl
    block = table.shape[1] // nr

    loads = {}
    sources = (res_hbm, visc_hbm, comp_hbm, ker_hbm, pres_hbm, therm_hbm, table_hbm, leg_hbm)
    targets = (res, visc, comp, ker, pres, therm, table, leg)
    names = ("res", "visc", "comp", "ker", "pres", "therm", "table", "leg")
    for i, (name, source, target) in enumerate(zip(names, sources, targets)):
        loads[name] = pltpu.make_async_copy(source, target, load_sem.at[i])
        loads[name].start()

    barrier = pltpu.get_barrier_semaphore()
    for d in range(1, nr):
        pl.semaphore_signal(barrier, inc=1, device_id={"radial": lax.rem(ri + d, nr)}, device_id_type=MESH)
    for d in range(1, nl):
        pl.semaphore_signal(barrier, inc=1, device_id={"lateral": lax.rem(li + d, nl)}, device_id_type=MESH)

    loads["res"].wait()
    r = [res[:, a, :] for a in range(cycles)]
    for a in range(cycles):
        shell_send[0, a : a + 1, :] = r[a][0:1]
        shell_send[1, a : a + 1, :] = r[a][shells - 1 : shells]
    cycle_send[0] = r[0]
    cycle_send[1] = r[cycles - 1]
    pl.semaphore_wait(barrier, nr - 1 + nl - 1)

    def edge(sender, receiver, ss, rs, slot, axis, target):
        return pltpu.make_async_remote_copy(
            src_ref=sender.at[slot], dst_ref=receiver.at[slot],
            send_sem=ss.at[slot], recv_sem=rs.at[slot],
            device_id={axis: target}, device_id_type=MESH,
        )

    sides = (
        (cycle_send, cycle_recv, cycle_ss, cycle_rs, "lateral", li, nl),
        (shell_send, shell_recv, shell_ss, shell_rs, "radial", ri, nr),
    )
    for sender, receiver, ss, rs, axis, me, n in sides:
        @pl.when(me > 0)
        def _():
            edge(sender, receiver, ss, rs, 0, axis, lax.rem(me + n - 1, n)).start()

        @pl.when(me < n - 1)
        def _():
            edge(sender, receiver, ss, rs, 1, axis, lax.rem(me + 1, n)).start()

    later = []
    loads["ker"].wait()
    ker_recv[0] = ker[...].astype(BF16)
    loads["comp"].wait()
    loads["visc"].wait()

    rows = lax.broadcasted_iota(jnp.int32, (shells, shells), 0)
    lanes = lax.broadcasted_iota(jnp.int32, (shells, shells), 1)
    spread = jnp.broadcast_to(comp[...], (shells, shells))
    scale = jnp.sum(jnp.where(rows == lanes, spread, 0.0), axis=1, keepdims=True)
    row = lax.broadcasted_iota(jnp.int32, (shells, nlon), 0)
    squares = None
    for a in range(cycles):
        term = folded(r[a] * r[a])
        squares = term if squares is None else squares + term

    for sender, receiver, ss, rs, axis, me, n in sides:
        @pl.when(me < n - 1)
        def _():
            edge(sender, receiver, ss, rs, 0, axis, lax.rem(me + 1, n)).wait_recv()

        @pl.when(me == n - 1)
        def _():
            receiver[0] = jnp.zeros(receiver.shape[1:], F32)

        @pl.when(me > 0)
        def _():
            edge(sender, receiver, ss, rs, 1, axis, lax.rem(me + n - 1, n)).wait_recv()

        @pl.when(me == 0)
        def _():
            receiver[1] = jnp.zeros(receiver.shape[1:], F32)

    image = []
    curvature = None
    for a in range(cycles):
        x = r[a]
        up = jnp.where(row == shells - 1, shell_recv[0, a : a + 1, :], pltpu.roll(x, shells - 1, 0))
        down = jnp.where(row == 0, shell_recv[1, a : a + 1, :], pltpu.roll(x, 1, 0))
        following = r[a + 1] if a + 1 < cycles else cycle_recv[0]
        preceding = r[a - 1] if a > 0 else cycle_recv[1]
        beside = up + down + following + preceding
        beside = beside + pltpu.roll(x, 1, 1) + pltpu.roll(x, nlon - 1, 1)
        y = (6.0 + visc[:, a, :]) * x - beside
        image.append(y)
        term = folded(x * y)
        curvature = term if curvature is None else curvature + term

    dot_r[0, 0:8] = squares
    dot_r[0, 8:16] = curvature
    copies = [
        send(dot_r.at[0], dot_r.at[d], dotr_ss.at[d], dotr_rs.at[d], "radial", lax.rem(ri + d, nr))
        for d in range(1, nr)
    ]
    later += copies
    ker_copies = [
        send(ker_recv.at[0], ker_recv.at[d], ker_ss.at[d], ker_rs.at[d], "radial", lax.rem(ri + d, nr))
        for d in range(1, nr)
    ]
    later += ker_copies
    for name in ("pres", "therm", "table", "leg"):
        loads[name].wait()
    for copy in copies:
        copy.wait_recv()
    total = dot_r[0]
    for d in range(1, nr):
        total = total + dot_r[d]
    dot_l[0] = total
    copies = [
        send(dot_l.at[0], dot_l.at[d], dotl_ss.at[d], dotl_rs.at[d], "lateral", lax.rem(li + d, nl))
        for d in range(1, nl)
    ]
    later += copies
    for copy in copies:
        copy.wait_recv()
    total = dot_l[0]
    for d in range(1, nl):
        total = total + dot_l[d]
    alpha = jnp.sum(total[0:8], keepdims=True) / jnp.sum(total[8:16], keepdims=True)

    anomaly, pressure_new = [], []
    for a in range(cycles):
        new = pres[:, a, :] + alpha * r[a]
        pressure_new.append(new)
        anomaly.append((therm[:, a, :] - scale * new).astype(BF16))
    spectrum = jnp.dot(jnp.concatenate(anomaly, axis=0), table[...], preferred_element_type=F32).astype(BF16)
    for b in range(nr):
        for a in range(cycles):
            spec_send[b, :, a * block : (a + 1) * block] = spectrum[
                a * shells : (a + 1) * shells, b * block : (b + 1) * block
            ]
    copies = []
    for d in range(1, nr):
        target = lax.rem(ri + d, nr)
        copies.append(send(spec_send.at[target], spec_recv.at[d], spec_ss.at[d], spec_rs.at[d], "radial", target))
    later += copies
    spec_recv[0] = spec_send[ri]
    for copy in ker_copies:
        copy.wait_recv()
    for k in range(2):
        whole = jnp.concatenate([ker_recv[d, k].astype(F32) for d in range(nr)], axis=0)
        ker_t[k] = whole.T.astype(BF16)
    for copy in copies:
        copy.wait_recv()

    stack = jnp.concatenate([spec_recv[d] for d in range(nr)], axis=0)
    first = pl.multiple_of(lax.rem(ri * block, orders), block)
    for k in range(2):
        weighted = jnp.dot(ker_t[k], stack, preferred_element_type=F32)
        value = None
        for a in range(cycles):
            term = weighted[:, a * block : (a + 1) * block] * leg[a, :, pl.ds(first, block)].astype(F32)
            value = term if value is None else value + term
        for b in range(nl):
            piece = value[b * owned : (b + 1) * owned]
            part[b, k * owned : (k + 1) * owned, :] = piece
            wire[b, k * owned : (k + 1) * owned, :] = piece.astype(wire.dtype)
    copies = []
    for d in range(1, nl):
        target = lax.rem(li + d, nl)
        copies.append(send(wire.at[target], terms.at[d], term_ss.at[d], term_rs.at[d], "lateral", target))
    later += copies
    for a in range(cycles):
        pres_out[:, a, :] = pressure_new[a]
        res_out[:, a, :] = r[a] - alpha * image[a]
    stores = [
        pltpu.make_async_copy(pres_out, pres_hbm_out, store_sem.at[0]),
        pltpu.make_async_copy(res_out, res_hbm_out, store_sem.at[1]),
    ]
    for store in stores:
        store.start()
    total = part[li]
    for d in range(1, nl):
        copies[d - 1].wait_recv()
        total = total + terms[d].astype(F32)
    mine = pl.ds(pl.multiple_of(ri * block, block), block)
    for k in range(2):
        final[k, :, mine] = total[k * owned : (k + 1) * owned]
    copies = [
        send(final.at[:, :, mine], final.at[:, :, mine], fin_ss.at[d], fin_rs.at[d], "radial", lax.rem(ri + d, nr))
        for d in range(1, nr)
    ]
    for d in range(1, nr):
        origin = lax.rem(ri + nr - d, nr)
        theirs = pl.ds(pl.multiple_of(origin * block, block), block)
        pltpu.make_async_remote_copy(
            src_ref=final.at[:, :, theirs], dst_ref=final.at[:, :, theirs],
            send_sem=fin_ss.at[d], recv_sem=fin_rs.at[d],
            device_id={"radial": origin}, device_id_type=MESH,
        ).wait_recv()
    for c in range(2):
        geoid_out[:, c, :] = final[0, :, c * orders : (c + 1) * orders]
        topo_out[:, c, :] = final[1, :, c * orders : (c + 1) * orders]
    responses = [
        pltpu.make_async_copy(geoid_out, geoid_hbm_out, store_sem.at[2]),
        pltpu.make_async_copy(topo_out, topo_hbm_out, store_sem.at[3]),
    ]
    for store in responses:
        store.start()
    for copy in later + copies:
        copy.wait_send()
    for store in stores + responses:
        store.wait()
    for sender, receiver, ss, rs, axis, me, n in sides:
        @pl.when(me > 0)
        def _():
            edge(sender, receiver, ss, rs, 0, axis, lax.rem(me + n - 1, n)).wait_send()

        @pl.when(me < n - 1)
        def _():
            edge(sender, receiver, ss, rs, 1, axis, lax.rem(me + 1, n)).wait_send()


def placed(*refs):
    sources, targets, sem = refs[:4], refs[4:8], refs[8]
    copies = [pltpu.make_async_copy(a, b, sem.at[i]) for i, (a, b) in enumerate(zip(sources, targets))]
    for copy in copies:
        copy.start()
    for copy in copies:
        copy.wait()


def on_device(pressure, residual, inv_visc, thermal, compress, legendre, kernels):
    nr, nl = lax.axis_size("radial"), lax.axis_size("lateral")
    shells, cycles, nlon = residual.shape
    degrees, orders = legendre.shape[1:]
    owned = degrees // nl
    block = 2 * orders // nr
    wire = BF16 if owned % 16 == 0 else F32
    table = jnp.asarray(fourier_table(nlon, orders))
    dma = pltpu.SemaphoreType.DMA
    anywhere = pl.BlockSpec(memory_space=pl.ANY)
    operands = (pressure, residual, inv_visc, thermal, compress[None, :], legendre, kernels, table)
    outputs = (
        jax.ShapeDtypeStruct(pressure.shape, F32),
        jax.ShapeDtypeStruct(residual.shape, F32),
        jax.ShapeDtypeStruct((owned, 2, orders), F32),
        jax.ShapeDtypeStruct((owned, 2, orders), F32),
    )
    results = pl.pallas_call(
        functools.partial(kernel, nr, nl),
        out_shape=outputs,
        in_specs=[anywhere] * 8,
        out_specs=(anywhere,) * 4,
        scratch_shapes=[
            *(pltpu.VMEM(x.shape, x.dtype) for x in operands),
            dma((8,)),
            pltpu.VMEM((2, owned, 2 * orders), F32),
            *(pltpu.VMEM(x.shape, x.dtype) for x in outputs),
            dma((4,)),
            pltpu.VMEM((2, cycles, nlon), F32),
            pltpu.VMEM((2, cycles, nlon), F32),
            pltpu.VMEM((2, shells, nlon), F32),
            pltpu.VMEM((2, shells, nlon), F32),
            pltpu.VMEM((nr, 16, 128), F32),
            pltpu.VMEM((nl, 16, 128), F32),
            pltpu.VMEM((nr, shells, cycles * block), BF16),
            pltpu.VMEM((nr, shells, cycles * block), BF16),
            pltpu.VMEM((nr, 2, shells, degrees), BF16),
            pltpu.VMEM((2, degrees, nr * shells), BF16),
            pltpu.VMEM((nl, 2 * owned, block), F32),
            pltpu.VMEM((nl, 2 * owned, block), wire),
            pltpu.VMEM((nl, 2 * owned, block), wire),
            dma((2,)), dma((2,)), dma((2,)), dma((2,)),
            dma((nr,)), dma((nr,)), dma((nl,)), dma((nl,)),
            dma((nr,)), dma((nr,)), dma((nr,)), dma((nr,)),
            dma((nl,)), dma((nl,)), dma((nr,)), dma((nr,)),
        ],
        compiler_params=pltpu.CompilerParams(
            collective_id=0, has_side_effects=True, vmem_limit_bytes=60 * 2**20
        ),
    )(*operands)
    return pl.pallas_call(
        placed,
        out_shape=outputs,
        in_specs=[anywhere] * 4,
        out_specs=(anywhere,) * 4,
        scratch_shapes=[dma((4,))],
        compiler_params=pltpu.CompilerParams(vmem_limit_bytes=60 * 2**20),
    )(*results)


def solution(mesh):
    return jax.shard_map(
        on_device,
        mesh=mesh,
        in_specs=(
            P("radial", "lateral", None),
            P("radial", "lateral", None),
            P("radial", "lateral", None),
            P("radial", "lateral", None),
            P("radial"),
            P("lateral", None, None),
            P(None, "radial", None),
        ),
        out_specs=(
            P("radial", "lateral", None),
            P("radial", "lateral", None),
            P("lateral", None, None),
            P("lateral", None, None),
        ),
        check_vma=False,
    )
```

```python
import functools
import math

import jax
import jax.numpy as jnp
import numpy as np
from jax import lax
from jax.experimental import pallas as pl
from jax.experimental.pallas import tpu as pltpu
from jax.sharding import PartitionSpec as P

MESH = pl.DeviceIdType.MESH
F32 = jnp.float32
BF16 = jnp.bfloat16


def fourier_table(nlon, orders):
    column = np.arange(nlon, dtype=np.int32)[:, None]
    order = np.arange(orders, dtype=np.int32)[None, :]
    phase = np.float32(2.0 * math.pi / nlon) * (column * order % nlon).astype(np.float32)
    scale = np.float32(1.0 / math.sqrt(nlon))
    return (np.concatenate([np.cos(phase), np.sin(phase)], axis=1) * scale).astype(BF16)


def send(src, dst, send_sem, recv_sem, axis, target):
    copy = pltpu.make_async_remote_copy(
        src_ref=src,
        dst_ref=dst,
        send_sem=send_sem,
        recv_sem=recv_sem,
        device_id={axis: target},
        device_id_type=MESH,
    )
    copy.start()
    return copy


def folded(x):
    rows = x.shape[0] // 8
    cols = x.shape[1] // 128
    total = None
    for i in range(rows):
        for j in range(cols):
            part = x[i * 8 : (i + 1) * 8, j * 128 : (j + 1) * 128]
            total = part if total is None else total + part
    return total


def kernel(
    nr, nl,
    pres_hbm, res_hbm, visc_hbm, therm_hbm, comp_hbm, leg_hbm, ker_hbm, table_hbm,
    pres_hbm_out, res_hbm_out, geoid_hbm_out, topo_hbm_out,
    pres, res, visc, therm, comp, leg, ker, table, load_sem, final,
    pres_out, res_out, geoid_out, topo_out, store_sem,
    shell_send, shell_recv, cycle_send, cycle_recv,
    dot_r, dot_l, spec_send, spec_recv, ker_recv, ker_t, part, wire, terms,
    shell_ss, shell_rs, cycle_ss, cycle_rs,
    dotr_ss, dotr_rs, dotl_ss, dotl_rs,
    spec_ss, spec_rs, ker_ss, ker_rs, term_ss, term_rs, fin_ss, fin_rs,
):
    ri, li = lax.axis_index("radial"), lax.axis_index("lateral")
    shells, cycles, nlon = res.shape
    degrees = leg.shape[1]
    orders = leg.shape[2]
    owned = degrees // nl
    block = table.shape[1] // nr

    loads = {}
    sources = (res_hbm, visc_hbm, comp_hbm, ker_hbm, pres_hbm, therm_hbm, table_hbm, leg_hbm)
    targets = (res, visc, comp, ker, pres, therm, table, leg)
    names = ("res", "visc", "comp", "ker", "pres", "therm", "table", "leg")
    for i, (name, source, target) in enumerate(zip(names, sources, targets)):
        loads[name] = pltpu.make_async_copy(source, target, load_sem.at[i])
        loads[name].start()

    barrier = pltpu.get_barrier_semaphore()
    for d in range(1, nr):
        pl.semaphore_signal(barrier, inc=1, device_id={"radial": lax.rem(ri + d, nr)}, device_id_type=MESH)
    for d in range(1, nl):
        pl.semaphore_signal(barrier, inc=1, device_id={"lateral": lax.rem(li + d, nl)}, device_id_type=MESH)

    loads["res"].wait()
    r = [res[:, a, :] for a in range(cycles)]
    for a in range(cycles):
        shell_send[0, a : a + 1, :] = r[a][0:1]
        shell_send[1, a : a + 1, :] = r[a][shells - 1 : shells]
    cycle_send[0] = r[0]
    cycle_send[1] = r[cycles - 1]
    pl.semaphore_wait(barrier, nr - 1 + nl - 1)

    def edge(sender, receiver, ss, rs, slot, axis, target):
        return pltpu.make_async_remote_copy(
            src_ref=sender.at[slot], dst_ref=receiver.at[slot],
            send_sem=ss.at[slot], recv_sem=rs.at[slot],
            device_id={axis: target}, device_id_type=MESH,
        )

    sides = (
        (cycle_send, cycle_recv, cycle_ss, cycle_rs, "lateral", li, nl),
        (shell_send, shell_recv, shell_ss, shell_rs, "radial", ri, nr),
    )
    for sender, receiver, ss, rs, axis, me, n in sides:
        @pl.when(me < n - 1)
        def _():
            edge(sender, receiver, ss, rs, 1, axis, lax.rem(me + 1, n)).start()

    later = []
    loads["ker"].wait()
    ker_recv[0] = ker[...].astype(BF16)
    loads["comp"].wait()
    loads["visc"].wait()

    rows = lax.broadcasted_iota(jnp.int32, (shells, shells), 0)
    lanes = lax.broadcasted_iota(jnp.int32, (shells, shells), 1)
    spread = jnp.broadcast_to(comp[...], (shells, shells))
    scale = jnp.sum(jnp.where(rows == lanes, spread, 0.0), axis=1, keepdims=True)
    row = lax.broadcasted_iota(jnp.int32, (shells, nlon), 0)
    squares = None
    for a in range(cycles):
        term = folded(r[a] * r[a])
        squares = term if squares is None else squares + term

    inner = []
    curvature = None
    for a in range(cycles):
        x = r[a]
        beside = jnp.where(row == shells - 1, 0.0, pltpu.roll(x, shells - 1, 0))
        beside = beside + jnp.where(row == 0, 0.0, pltpu.roll(x, 1, 0))
        if a + 1 < cycles:
            beside = beside + r[a + 1]
        if a > 0:
            beside = beside + r[a - 1]
        beside = beside + pltpu.roll(x, 1, 1) + pltpu.roll(x, nlon - 1, 1)
        y = (6.0 + visc[:, a, :]) * x - beside
        inner.append(y)
        term = folded(x * y)
        curvature = term if curvature is None else curvature + term

    for sender, receiver, ss, rs, axis, me, n in sides:
        @pl.when(me > 0)
        def _():
            edge(sender, receiver, ss, rs, 1, axis, lax.rem(me + n - 1, n)).wait_recv()

        @pl.when(me == 0)
        def _():
            receiver[1] = jnp.zeros(receiver.shape[1:], F32)

    across = folded(r[0] * cycle_recv[1])
    for a in range(cycles):
        across = across + folded(r[a][0:8] * jnp.where(row[0:8] == 0, shell_recv[1, a : a + 1, :], 0.0))
    curvature = curvature - 2.0 * across

    dot_r[0, 0:8] = squares
    dot_r[0, 8:16] = curvature
    copies = [
        send(dot_r.at[0], dot_r.at[d], dotr_ss.at[d], dotr_rs.at[d], "radial", lax.rem(ri + d, nr))
        for d in range(1, nr)
    ]
    later += copies
    ker_copies = [
        send(ker_recv.at[0], ker_recv.at[d], ker_ss.at[d], ker_rs.at[d], "radial", lax.rem(ri + d, nr))
        for d in range(1, nr)
    ]
    later += ker_copies
    for name in ("pres", "therm", "table", "leg"):
        loads[name].wait()
    for copy in copies:
        copy.wait_recv()
    total = dot_r[0]
    for d in range(1, nr):
        total = total + dot_r[d]
    dot_l[0] = total
    copies = [
        send(dot_l.at[0], dot_l.at[d], dotl_ss.at[d], dotl_rs.at[d], "lateral", lax.rem(li + d, nl))
        for d in range(1, nl)
    ]
    later += copies
    for sender, receiver, ss, rs, axis, me, n in sides:
        @pl.when(me > 0)
        def _():
            edge(sender, receiver, ss, rs, 0, axis, lax.rem(me + n - 1, n)).start()

    for copy in copies:
        copy.wait_recv()
    total = dot_l[0]
    for d in range(1, nl):
        total = total + dot_l[d]
    alpha = jnp.sum(total[0:8], keepdims=True) / jnp.sum(total[8:16], keepdims=True)

    anomaly, pressure_new = [], []
    for a in range(cycles):
        new = pres[:, a, :] + alpha * r[a]
        pressure_new.append(new)
        anomaly.append((therm[:, a, :] - scale * new).astype(BF16))
    spectrum = jnp.dot(jnp.concatenate(anomaly, axis=0), table[...], preferred_element_type=F32).astype(BF16)
    for b in range(nr):
        for a in range(cycles):
            spec_send[b, :, a * block : (a + 1) * block] = spectrum[
                a * shells : (a + 1) * shells, b * block : (b + 1) * block
            ]
    copies = []
    for d in range(1, nr):
        target = lax.rem(ri + d, nr)
        copies.append(send(spec_send.at[target], spec_recv.at[d], spec_ss.at[d], spec_rs.at[d], "radial", target))
    later += copies
    spec_recv[0] = spec_send[ri]
    for copy in ker_copies:
        copy.wait_recv()
    for k in range(2):
        whole = jnp.concatenate([ker_recv[d, k].astype(F32) for d in range(nr)], axis=0)
        ker_t[k] = whole.T.astype(BF16)
    for copy in copies:
        copy.wait_recv()

    stack = jnp.concatenate([spec_recv[d] for d in range(nr)], axis=0)
    first = pl.multiple_of(lax.rem(ri * block, orders), block)
    for k in range(2):
        weighted = jnp.dot(ker_t[k], stack, preferred_element_type=F32)
        value = None
        for a in range(cycles):
            term = weighted[:, a * block : (a + 1) * block] * leg[a, :, pl.ds(first, block)].astype(F32)
            value = term if value is None else value + term
        for b in range(nl):
            piece = value[b * owned : (b + 1) * owned]
            part[b, k * owned : (k + 1) * owned, :] = piece
            wire[b, k * owned : (k + 1) * owned, :] = piece.astype(wire.dtype)
    copies = []
    for d in range(1, nl):
        target = lax.rem(li + d, nl)
        copies.append(send(wire.at[target], terms.at[d], term_ss.at[d], term_rs.at[d], "lateral", target))
    later += copies
    for sender, receiver, ss, rs, axis, me, n in sides:
        @pl.when(me < n - 1)
        def _():
            edge(sender, receiver, ss, rs, 0, axis, lax.rem(me + 1, n)).wait_recv()

        @pl.when(me == n - 1)
        def _():
            receiver[0] = jnp.zeros(receiver.shape[1:], F32)

    for a in range(cycles):
        image = inner[a] - jnp.where(row == shells - 1, shell_recv[0, a : a + 1, :], 0.0)
        image = image - jnp.where(row == 0, shell_recv[1, a : a + 1, :], 0.0)
        if a == 0:
            image = image - cycle_recv[1]
        if a == cycles - 1:
            image = image - cycle_recv[0]
        pres_out[:, a, :] = pressure_new[a]
        res_out[:, a, :] = r[a] - alpha * image
    stores = [
        pltpu.make_async_copy(pres_out, pres_hbm_out, store_sem.at[0]),
        pltpu.make_async_copy(res_out, res_hbm_out, store_sem.at[1]),
    ]
    for store in stores:
        store.start()
    total = part[li]
    for d in range(1, nl):
        copies[d - 1].wait_recv()
        total = total + terms[d].astype(F32)
    mine = pl.ds(pl.multiple_of(ri * block, block), block)
    for k in range(2):
        final[k, :, mine] = total[k * owned : (k + 1) * owned]
    copies = [
        send(final.at[:, :, mine], final.at[:, :, mine], fin_ss.at[d], fin_rs.at[d], "radial", lax.rem(ri + d, nr))
        for d in range(1, nr)
    ]
    for d in range(1, nr):
        origin = lax.rem(ri + nr - d, nr)
        theirs = pl.ds(pl.multiple_of(origin * block, block), block)
        pltpu.make_async_remote_copy(
            src_ref=final.at[:, :, theirs], dst_ref=final.at[:, :, theirs],
            send_sem=fin_ss.at[d], recv_sem=fin_rs.at[d],
            device_id={"radial": origin}, device_id_type=MESH,
        ).wait_recv()
    for c in range(2):
        geoid_out[:, c, :] = final[0, :, c * orders : (c + 1) * orders]
        topo_out[:, c, :] = final[1, :, c * orders : (c + 1) * orders]
    responses = [
        pltpu.make_async_copy(geoid_out, geoid_hbm_out, store_sem.at[2]),
        pltpu.make_async_copy(topo_out, topo_hbm_out, store_sem.at[3]),
    ]
    for store in responses:
        store.start()
    for copy in later + copies:
        copy.wait_send()
    for store in stores + responses:
        store.wait()
    for sender, receiver, ss, rs, axis, me, n in sides:
        @pl.when(me > 0)
        def _():
            edge(sender, receiver, ss, rs, 0, axis, lax.rem(me + n - 1, n)).wait_send()

        @pl.when(me < n - 1)
        def _():
            edge(sender, receiver, ss, rs, 1, axis, lax.rem(me + 1, n)).wait_send()


def placed(*refs):
    sources, targets, held, load_sem, store_sem = refs[:4], refs[4:8], refs[8:12], refs[12], refs[13]
    loads = [pltpu.make_async_copy(a, b, load_sem.at[i]) for i, (a, b) in enumerate(zip(sources, held))]
    stores = [pltpu.make_async_copy(a, b, store_sem.at[i]) for i, (a, b) in enumerate(zip(held, targets))]
    for load in loads:
        load.start()
    for load, store in zip(loads, stores):
        load.wait()
        store.start()
    for store in stores:
        store.wait()


def on_device(pressure, residual, inv_visc, thermal, compress, legendre, kernels):
    nr, nl = lax.axis_size("radial"), lax.axis_size("lateral")
    shells, cycles, nlon = residual.shape
    degrees, orders = legendre.shape[1:]
    owned = degrees // nl
    block = 2 * orders // nr
    wire = BF16 if owned % 16 == 0 else F32
    table = jnp.asarray(fourier_table(nlon, orders))
    dma = pltpu.SemaphoreType.DMA
    anywhere = pl.BlockSpec(memory_space=pl.ANY)
    operands = (pressure, residual, inv_visc, thermal, compress[None, :], legendre, kernels, table)
    outputs = (
        jax.ShapeDtypeStruct(pressure.shape, F32),
        jax.ShapeDtypeStruct(residual.shape, F32),
        jax.ShapeDtypeStruct((owned, 2, orders), F32),
        jax.ShapeDtypeStruct((owned, 2, orders), F32),
    )
    results = pl.pallas_call(
        functools.partial(kernel, nr, nl),
        out_shape=outputs,
        in_specs=[anywhere] * 8,
        out_specs=(anywhere,) * 4,
        scratch_shapes=[
            *(pltpu.VMEM(x.shape, x.dtype) for x in operands),
            dma((8,)),
            pltpu.VMEM((2, owned, 2 * orders), F32),
            *(pltpu.VMEM(x.shape, x.dtype) for x in outputs),
            dma((4,)),
            pltpu.VMEM((2, cycles, nlon), F32),
            pltpu.VMEM((2, cycles, nlon), F32),
            pltpu.VMEM((2, shells, nlon), F32),
            pltpu.VMEM((2, shells, nlon), F32),
            pltpu.VMEM((nr, 16, 128), F32),
            pltpu.VMEM((nl, 16, 128), F32),
            pltpu.VMEM((nr, shells, cycles * block), BF16),
            pltpu.VMEM((nr, shells, cycles * block), BF16),
            pltpu.VMEM((nr, 2, shells, degrees), BF16),
            pltpu.VMEM((2, degrees, nr * shells), BF16),
            pltpu.VMEM((nl, 2 * owned, block), F32),
            pltpu.VMEM((nl, 2 * owned, block), wire),
            pltpu.VMEM((nl, 2 * owned, block), wire),
            dma((2,)), dma((2,)), dma((2,)), dma((2,)),
            dma((nr,)), dma((nr,)), dma((nl,)), dma((nl,)),
            dma((nr,)), dma((nr,)), dma((nr,)), dma((nr,)),
            dma((nl,)), dma((nl,)), dma((nr,)), dma((nr,)),
        ],
        compiler_params=pltpu.CompilerParams(
            collective_id=0, has_side_effects=True, vmem_limit_bytes=60 * 2**20
        ),
    )(*operands)
    return pl.pallas_call(
        placed,
        out_shape=outputs,
        in_specs=[anywhere] * 4,
        out_specs=(anywhere,) * 4,
        scratch_shapes=[*(pltpu.VMEM(x.shape, x.dtype) for x in outputs), dma((4,)), dma((4,))],
        compiler_params=pltpu.CompilerParams(vmem_limit_bytes=60 * 2**20),
    )(*results)


def solution(mesh):
    return jax.shard_map(
        on_device,
        mesh=mesh,
        in_specs=(
            P("radial", "lateral", None),
            P("radial", "lateral", None),
            P("radial", "lateral", None),
            P("radial", "lateral", None),
            P("radial"),
            P("lateral", None, None),
            P(None, "radial", None),
        ),
        out_specs=(
            P("radial", "lateral", None),
            P("radial", "lateral", None),
            P("lateral", None, None),
            P("lateral", None, None),
        ),
        check_vma=False,
    )
```

```python
import functools
import math

import jax
import jax.numpy as jnp
import numpy as np
from jax import lax
from jax.experimental import pallas as pl
from jax.experimental.pallas import tpu as pltpu
from jax.sharding import PartitionSpec as P

MESH = pl.DeviceIdType.MESH
F32 = jnp.float32
BF16 = jnp.bfloat16


def fourier_table(nlon, orders):
    column = np.arange(nlon, dtype=np.int32)[:, None]
    order = np.arange(orders, dtype=np.int32)[None, :]
    phase = np.float32(2.0 * math.pi / nlon) * (column * order % nlon).astype(np.float32)
    scale = np.float32(1.0 / math.sqrt(nlon))
    return (np.concatenate([np.cos(phase), np.sin(phase)], axis=1) * scale).astype(BF16)


def send(src, dst, send_sem, recv_sem, axis, target):
    copy = pltpu.make_async_remote_copy(
        src_ref=src,
        dst_ref=dst,
        send_sem=send_sem,
        recv_sem=recv_sem,
        device_id={axis: target},
        device_id_type=MESH,
    )
    copy.start()
    return copy


def folded(x):
    rows = x.shape[0] // 8
    cols = x.shape[1] // 128
    total = None
    for i in range(rows):
        for j in range(cols):
            part = x[i * 8 : (i + 1) * 8, j * 128 : (j + 1) * 128]
            total = part if total is None else total + part
    return total


def kernel(
    nr, nl,
    pres_hbm, res_hbm, visc_hbm, therm_hbm, comp_hbm, leg_hbm, ker_hbm, table_hbm,
    pres_hbm_out, res_hbm_out, geoid_hbm_out, topo_hbm_out,
    pres, res, visc, therm, comp, leg, ker, table, load_sem, final,
    pres_out, res_out, geoid_out, topo_out, store_sem,
    shell_send, shell_recv, cycle_send, cycle_recv,
    dot_r, dot_l, spec_send, spec_recv, ker_recv, ker_t, part, wire, terms,
    shell_ss, shell_rs, cycle_ss, cycle_rs,
    dotr_ss, dotr_rs, dotl_ss, dotl_rs,
    spec_ss, spec_rs, ker_ss, ker_rs, term_ss, term_rs, fin_ss, fin_rs,
):
    ri, li = lax.axis_index("radial"), lax.axis_index("lateral")
    shells, cycles, nlon = res.shape
    degrees = leg.shape[1]
    orders = leg.shape[2]
    owned = degrees // nl
    block = table.shape[1] // nr

    loads = {}
    sources = (res_hbm, visc_hbm, comp_hbm, ker_hbm, pres_hbm, therm_hbm, table_hbm, leg_hbm)
    targets = (res, visc, comp, ker, pres, therm, table, leg)
    names = ("res", "visc", "comp", "ker", "pres", "therm", "table", "leg")
    for i, (name, source, target) in enumerate(zip(names, sources, targets)):
        loads[name] = pltpu.make_async_copy(source, target, load_sem.at[i])
        loads[name].start()

    barrier = pltpu.get_barrier_semaphore()
    for d in range(1, nr):
        pl.semaphore_signal(barrier, inc=1, device_id={"radial": lax.rem(ri + d, nr)}, device_id_type=MESH)
    for d in range(1, nl):
        pl.semaphore_signal(barrier, inc=1, device_id={"lateral": lax.rem(li + d, nl)}, device_id_type=MESH)

    loads["res"].wait()
    r = [res[:, a, :] for a in range(cycles)]
    for a in range(cycles):
        shell_send[0, a : a + 1, :] = r[a][0:1]
        shell_send[1, a : a + 1, :] = r[a][shells - 1 : shells]
    cycle_send[0] = r[0]
    cycle_send[1] = r[cycles - 1]
    pl.semaphore_wait(barrier, nr - 1 + nl - 1)

    def edge(sender, receiver, ss, rs, slot, axis, target):
        return pltpu.make_async_remote_copy(
            src_ref=sender.at[slot], dst_ref=receiver.at[slot],
            send_sem=ss.at[slot], recv_sem=rs.at[slot],
            device_id={axis: target}, device_id_type=MESH,
        )

    sides = (
        (cycle_send, cycle_recv, cycle_ss, cycle_rs, "lateral", li, nl),
        (shell_send, shell_recv, shell_ss, shell_rs, "radial", ri, nr),
    )
    for sender, receiver, ss, rs, axis, me, n in sides:
        @pl.when(me < n - 1)
        def _():
            edge(sender, receiver, ss, rs, 1, axis, lax.rem(me + 1, n)).start()

    later = []
    loads["ker"].wait()
    ker_recv[0] = ker[...].astype(BF16)
    loads["comp"].wait()
    loads["visc"].wait()

    rows = lax.broadcasted_iota(jnp.int32, (shells, shells), 0)
    lanes = lax.broadcasted_iota(jnp.int32, (shells, shells), 1)
    spread = jnp.broadcast_to(comp[...], (shells, shells))
    scale = jnp.sum(jnp.where(rows == lanes, spread, 0.0), axis=1, keepdims=True)
    row = lax.broadcasted_iota(jnp.int32, (shells, nlon), 0)
    squares = None
    for a in range(cycles):
        term = folded(r[a] * r[a])
        squares = term if squares is None else squares + term

    inner = []
    curvature = None
    for a in range(cycles):
        x = r[a]
        beside = jnp.where(row == shells - 1, 0.0, pltpu.roll(x, shells - 1, 0))
        beside = beside + jnp.where(row == 0, 0.0, pltpu.roll(x, 1, 0))
        if a + 1 < cycles:
            beside = beside + r[a + 1]
        if a > 0:
            beside = beside + r[a - 1]
        beside = beside + pltpu.roll(x, 1, 1) + pltpu.roll(x, nlon - 1, 1)
        y = (6.0 + visc[:, a, :]) * x - beside
        inner.append(y)
        term = folded(x * y)
        curvature = term if curvature is None else curvature + term

    for sender, receiver, ss, rs, axis, me, n in sides:
        @pl.when(me > 0)
        def _():
            edge(sender, receiver, ss, rs, 1, axis, lax.rem(me + n - 1, n)).wait_recv()

        @pl.when(me == 0)
        def _():
            receiver[1] = jnp.zeros(receiver.shape[1:], F32)

    across = folded(r[0] * cycle_recv[1])
    for a in range(cycles):
        across = across + folded(r[a][0:8] * jnp.where(row[0:8] == 0, shell_recv[1, a : a + 1, :], 0.0))
    curvature = curvature - 2.0 * across

    dot_r[0, 0:1] = jnp.sum(squares, axis=0, keepdims=True)
    dot_r[0, 1:2] = jnp.sum(curvature, axis=0, keepdims=True)
    copies = [
        send(dot_r.at[0], dot_r.at[d], dotr_ss.at[d], dotr_rs.at[d], "radial", lax.rem(ri + d, nr))
        for d in range(1, nr)
    ]
    later += copies
    ker_copies = [
        send(ker_recv.at[0], ker_recv.at[d], ker_ss.at[d], ker_rs.at[d], "radial", lax.rem(ri + d, nr))
        for d in range(1, nr)
    ]
    later += ker_copies
    for name in ("pres", "therm", "table", "leg"):
        loads[name].wait()
    for copy in copies:
        copy.wait_recv()
    total = dot_r[0]
    for d in range(1, nr):
        total = total + dot_r[d]
    dot_l[0] = total
    copies = [
        send(dot_l.at[0], dot_l.at[d], dotl_ss.at[d], dotl_rs.at[d], "lateral", lax.rem(li + d, nl))
        for d in range(1, nl)
    ]
    later += copies
    for sender, receiver, ss, rs, axis, me, n in sides:
        @pl.when(me > 0)
        def _():
            edge(sender, receiver, ss, rs, 0, axis, lax.rem(me + n - 1, n)).start()

    for copy in copies:
        copy.wait_recv()
    total = dot_l[0]
    for d in range(1, nl):
        total = total + dot_l[d]
    alpha = jnp.sum(total[0:1], keepdims=True) / jnp.sum(total[1:2], keepdims=True)

    anomaly, pressure_new = [], []
    for a in range(cycles):
        new = pres[:, a, :] + alpha * r[a]
        pressure_new.append(new)
        anomaly.append((therm[:, a, :] - scale * new).astype(BF16))
    spectrum = jnp.dot(jnp.concatenate(anomaly, axis=0), table[...], preferred_element_type=F32).astype(BF16)
    for b in range(nr):
        for a in range(cycles):
            spec_send[b, :, a * block : (a + 1) * block] = spectrum[
                a * shells : (a + 1) * shells, b * block : (b + 1) * block
            ]
    copies = []
    for d in range(1, nr):
        target = lax.rem(ri + d, nr)
        copies.append(send(spec_send.at[target], spec_recv.at[d], spec_ss.at[d], spec_rs.at[d], "radial", target))
    later += copies
    spec_recv[0] = spec_send[ri]
    for copy in ker_copies:
        copy.wait_recv()
    for k in range(2):
        whole = jnp.concatenate([ker_recv[d, k].astype(F32) for d in range(nr)], axis=0)
        ker_t[k] = whole.T.astype(BF16)
    for copy in copies:
        copy.wait_recv()

    stack = jnp.concatenate([spec_recv[d] for d in range(nr)], axis=0)
    first = pl.multiple_of(lax.rem(ri * block, orders), block)
    for k in range(2):
        weighted = jnp.dot(ker_t[k], stack, preferred_element_type=F32)
        value = None
        for a in range(cycles):
            term = weighted[:, a * block : (a + 1) * block] * leg[a, :, pl.ds(first, block)].astype(F32)
            value = term if value is None else value + term
        for b in range(nl):
            piece = value[b * owned : (b + 1) * owned]
            part[b, k * owned : (k + 1) * owned, :] = piece
            wire[b, k * owned : (k + 1) * owned, :] = piece.astype(wire.dtype)
    far_first = sorted(range(1, nl), key=lambda d: -min(d, nl - d))
    copies = []
    for d in far_first:
        target = lax.rem(li + d, nl)
        copies.append(send(wire.at[target], terms.at[d], term_ss.at[d], term_rs.at[d], "lateral", target))
    later += copies
    for sender, receiver, ss, rs, axis, me, n in sides:
        @pl.when(me < n - 1)
        def _():
            edge(sender, receiver, ss, rs, 0, axis, lax.rem(me + 1, n)).wait_recv()

        @pl.when(me == n - 1)
        def _():
            receiver[0] = jnp.zeros(receiver.shape[1:], F32)

    for a in range(cycles):
        image = inner[a] - jnp.where(row == shells - 1, shell_recv[0, a : a + 1, :], 0.0)
        image = image - jnp.where(row == 0, shell_recv[1, a : a + 1, :], 0.0)
        if a == 0:
            image = image - cycle_recv[1]
        if a == cycles - 1:
            image = image - cycle_recv[0]
        pres_out[:, a, :] = pressure_new[a]
        res_out[:, a, :] = r[a] - alpha * image
    stores = [
        pltpu.make_async_copy(pres_out, pres_hbm_out, store_sem.at[0]),
        pltpu.make_async_copy(res_out, res_hbm_out, store_sem.at[1]),
    ]
    for store in stores:
        store.start()
    total = part[li]
    for d, copy in zip(far_first, copies):
        copy.wait_recv()
        total = total + terms[d].astype(F32)
    mine = pl.ds(pl.multiple_of(ri * block, block), block)
    for k in range(2):
        final[k, :, mine] = total[k * owned : (k + 1) * owned].astype(final.dtype)
    copies = [
        send(final.at[:, :, mine], final.at[:, :, mine], fin_ss.at[d], fin_rs.at[d], "radial", lax.rem(ri + d, nr))
        for d in range(1, nr)
    ]
    for d in range(1, nr):
        origin = lax.rem(ri + nr - d, nr)
        theirs = pl.ds(pl.multiple_of(origin * block, block), block)
        pltpu.make_async_remote_copy(
            src_ref=final.at[:, :, theirs], dst_ref=final.at[:, :, theirs],
            send_sem=fin_ss.at[d], recv_sem=fin_rs.at[d],
            device_id={"radial": origin}, device_id_type=MESH,
        ).wait_recv()
    for c in range(2):
        geoid_out[:, c, :] = final[0, :, c * orders : (c + 1) * orders].astype(F32)
        topo_out[:, c, :] = final[1, :, c * orders : (c + 1) * orders].astype(F32)
    responses = [
        pltpu.make_async_copy(geoid_out, geoid_hbm_out, store_sem.at[2]),
        pltpu.make_async_copy(topo_out, topo_hbm_out, store_sem.at[3]),
    ]
    for store in responses:
        store.start()
    for copy in later + copies:
        copy.wait_send()
    for store in stores + responses:
        store.wait()
    for sender, receiver, ss, rs, axis, me, n in sides:
        @pl.when(me > 0)
        def _():
            edge(sender, receiver, ss, rs, 0, axis, lax.rem(me + n - 1, n)).wait_send()

        @pl.when(me < n - 1)
        def _():
            edge(sender, receiver, ss, rs, 1, axis, lax.rem(me + 1, n)).wait_send()


def placed(*refs):
    sources, targets, held, load_sem, store_sem = refs[:4], refs[4:8], refs[8:12], refs[12], refs[13]
    loads = [pltpu.make_async_copy(a, b, load_sem.at[i]) for i, (a, b) in enumerate(zip(sources, held))]
    stores = [pltpu.make_async_copy(a, b, store_sem.at[i]) for i, (a, b) in enumerate(zip(held, targets))]
    for load in loads:
        load.start()
    for load, store in zip(loads, stores):
        load.wait()
        store.start()
    for store in stores:
        store.wait()


def on_device(pressure, residual, inv_visc, thermal, compress, legendre, kernels):
    nr, nl = lax.axis_size("radial"), lax.axis_size("lateral")
    shells, cycles, nlon = residual.shape
    degrees, orders = legendre.shape[1:]
    owned = degrees // nl
    block = 2 * orders // nr
    wire = BF16 if owned % 16 == 0 else F32
    table = jnp.asarray(fourier_table(nlon, orders))
    dma = pltpu.SemaphoreType.DMA
    anywhere = pl.BlockSpec(memory_space=pl.ANY)
    operands = (pressure, residual, inv_visc, thermal, compress[None, :], legendre, kernels, table)
    outputs = (
        jax.ShapeDtypeStruct(pressure.shape, F32),
        jax.ShapeDtypeStruct(residual.shape, F32),
        jax.ShapeDtypeStruct((owned, 2, orders), F32),
        jax.ShapeDtypeStruct((owned, 2, orders), F32),
    )
    results = pl.pallas_call(
        functools.partial(kernel, nr, nl),
        out_shape=outputs,
        in_specs=[anywhere] * 8,
        out_specs=(anywhere,) * 4,
        scratch_shapes=[
            *(pltpu.VMEM(x.shape, x.dtype) for x in operands),
            dma((8,)),
            pltpu.VMEM((2, owned, 2 * orders), wire),
            *(pltpu.VMEM(x.shape, x.dtype) for x in outputs),
            dma((4,)),
            pltpu.VMEM((2, cycles, nlon), F32),
            pltpu.VMEM((2, cycles, nlon), F32),
            pltpu.VMEM((2, shells, nlon), F32),
            pltpu.VMEM((2, shells, nlon), F32),
            pltpu.VMEM((nr, 2, 128), F32),
            pltpu.VMEM((nl, 2, 128), F32),
            pltpu.VMEM((nr, shells, cycles * block), BF16),
            pltpu.VMEM((nr, shells, cycles * block), BF16),
            pltpu.VMEM((nr, 2, shells, degrees), BF16),
            pltpu.VMEM((2, degrees, nr * shells), BF16),
            pltpu.VMEM((nl, 2 * owned, block), F32),
            pltpu.VMEM((nl, 2 * owned, block), wire),
            pltpu.VMEM((nl, 2 * owned, block), wire),
            dma((2,)), dma((2,)), dma((2,)), dma((2,)),
            dma((nr,)), dma((nr,)), dma((nl,)), dma((nl,)),
            dma((nr,)), dma((nr,)), dma((nr,)), dma((nr,)),
            dma((nl,)), dma((nl,)), dma((nr,)), dma((nr,)),
        ],
        compiler_params=pltpu.CompilerParams(
            collective_id=0, has_side_effects=True, vmem_limit_bytes=60 * 2**20
        ),
    )(*operands)
    return pl.pallas_call(
        placed,
        out_shape=outputs,
        in_specs=[anywhere] * 4,
        out_specs=(anywhere,) * 4,
        scratch_shapes=[*(pltpu.VMEM(x.shape, x.dtype) for x in outputs), dma((4,)), dma((4,))],
        compiler_params=pltpu.CompilerParams(vmem_limit_bytes=60 * 2**20),
    )(*results)


def solution(mesh):
    return jax.shard_map(
        on_device,
        mesh=mesh,
        in_specs=(
            P("radial", "lateral", None),
            P("radial", "lateral", None),
            P("radial", "lateral", None),
            P("radial", "lateral", None),
            P("radial"),
            P("lateral", None, None),
            P(None, "radial", None),
        ),
        out_specs=(
            P("radial", "lateral", None),
            P("radial", "lateral", None),
            P("lateral", None, None),
            P("lateral", None, None),
        ),
        check_vma=False,
    )
```

```python
import functools
import math

import jax
import jax.numpy as jnp
import numpy as np
from jax import lax
from jax.experimental import pallas as pl
from jax.experimental.pallas import tpu as pltpu
from jax.sharding import PartitionSpec as P

MESH = pl.DeviceIdType.MESH
F32 = jnp.float32
BF16 = jnp.bfloat16


def fourier_table(nlon, orders):
    column = np.arange(nlon, dtype=np.int32)[:, None]
    order = np.arange(orders, dtype=np.int32)[None, :]
    phase = np.float32(2.0 * math.pi / nlon) * (column * order % nlon).astype(np.float32)
    scale = np.float32(1.0 / math.sqrt(nlon))
    return (np.concatenate([np.cos(phase), np.sin(phase)], axis=1) * scale).astype(BF16)


def send(src, dst, send_sem, recv_sem, axis, target):
    copy = pltpu.make_async_remote_copy(
        src_ref=src,
        dst_ref=dst,
        send_sem=send_sem,
        recv_sem=recv_sem,
        device_id={axis: target},
        device_id_type=MESH,
    )
    copy.start()
    return copy


def folded(x):
    rows = x.shape[0] // 8
    cols = x.shape[1] // 128
    total = None
    for i in range(rows):
        for j in range(cols):
            part = x[i * 8 : (i + 1) * 8, j * 128 : (j + 1) * 128]
            total = part if total is None else total + part
    return total


def kernel(
    nr, nl,
    pres_hbm, res_hbm, visc_hbm, therm_hbm, comp_hbm, leg_hbm, ker_hbm, table_hbm,
    pres_hbm_out, res_hbm_out, geoid_hbm_out, topo_hbm_out,
    pres, res, visc, therm, comp, leg, ker, table, load_sem, final,
    pres_out, res_out, geoid_out, topo_out, store_sem,
    shell_send, shell_recv, cycle_send, cycle_recv,
    dot_r, dot_l, spec_send, spec_recv, ker_recv, ker_t, part, wire, terms,
    shell_ss, shell_rs, cycle_ss, cycle_rs,
    dotr_ss, dotr_rs, dotl_ss, dotl_rs,
    spec_ss, spec_rs, ker_ss, ker_rs, term_ss, term_rs, fin_ss, fin_rs,
):
    ri, li = lax.axis_index("radial"), lax.axis_index("lateral")
    shells, cycles, nlon = res.shape
    degrees = leg.shape[1]
    orders = leg.shape[2]
    owned = degrees // nl
    block = table.shape[1] // nr

    loads = {}
    sources = (res_hbm, visc_hbm, comp_hbm, ker_hbm, pres_hbm, therm_hbm, table_hbm, leg_hbm)
    targets = (res, visc, comp, ker, pres, therm, table, leg)
    names = ("res", "visc", "comp", "ker", "pres", "therm", "table", "leg")
    for i, (name, source, target) in enumerate(zip(names, sources, targets)):
        loads[name] = pltpu.make_async_copy(source, target, load_sem.at[i])
        loads[name].start()

    barrier = pltpu.get_barrier_semaphore()
    for d in range(1, nr):
        pl.semaphore_signal(barrier, inc=1, device_id={"radial": lax.rem(ri + d, nr)}, device_id_type=MESH)
    for d in range(1, nl):
        pl.semaphore_signal(barrier, inc=1, device_id={"lateral": lax.rem(li + d, nl)}, device_id_type=MESH)

    loads["res"].wait()
    r = [res[:, a, :] for a in range(cycles)]
    for a in range(cycles):
        shell_send[0, a : a + 1, :] = r[a][0:1]
        shell_send[1, a : a + 1, :] = r[a][shells - 1 : shells]
    cycle_send[0] = r[0]
    cycle_send[1] = r[cycles - 1]
    pl.semaphore_wait(barrier, nr - 1 + nl - 1)

    def edge(sender, receiver, ss, rs, slot, axis, target):
        return pltpu.make_async_remote_copy(
            src_ref=sender.at[slot], dst_ref=receiver.at[slot],
            send_sem=ss.at[slot], recv_sem=rs.at[slot],
            device_id={axis: target}, device_id_type=MESH,
        )

    sides = (
        (cycle_send, cycle_recv, cycle_ss, cycle_rs, "lateral", li, nl),
        (shell_send, shell_recv, shell_ss, shell_rs, "radial", ri, nr),
    )
    for sender, receiver, ss, rs, axis, me, n in sides:
        @pl.when(me < n - 1)
        def _():
            edge(sender, receiver, ss, rs, 1, axis, lax.rem(me + 1, n)).start()

    later = []
    loads["ker"].wait()
    ker_recv[0] = ker[...].astype(BF16)
    loads["comp"].wait()
    loads["visc"].wait()

    rows = lax.broadcasted_iota(jnp.int32, (shells, shells), 0)
    lanes = lax.broadcasted_iota(jnp.int32, (shells, shells), 1)
    spread = jnp.broadcast_to(comp[...], (shells, shells))
    scale = jnp.sum(jnp.where(rows == lanes, spread, 0.0), axis=1, keepdims=True)
    row = lax.broadcasted_iota(jnp.int32, (shells, nlon), 0)
    squares = None
    for a in range(cycles):
        term = folded(r[a] * r[a])
        squares = term if squares is None else squares + term

    inner = []
    curvature = None
    for a in range(cycles):
        x = r[a]
        beside = jnp.where(row == shells - 1, 0.0, pltpu.roll(x, shells - 1, 0))
        beside = beside + jnp.where(row == 0, 0.0, pltpu.roll(x, 1, 0))
        if a + 1 < cycles:
            beside = beside + r[a + 1]
        if a > 0:
            beside = beside + r[a - 1]
        beside = beside + pltpu.roll(x, 1, 1) + pltpu.roll(x, nlon - 1, 1)
        y = (6.0 + visc[:, a, :]) * x - beside
        inner.append(y)
        term = folded(x * y)
        curvature = term if curvature is None else curvature + term

    for sender, receiver, ss, rs, axis, me, n in sides:
        @pl.when(me > 0)
        def _():
            edge(sender, receiver, ss, rs, 1, axis, lax.rem(me + n - 1, n)).wait_recv()

        @pl.when(me == 0)
        def _():
            receiver[1] = jnp.zeros(receiver.shape[1:], F32)

    across = folded(r[0] * cycle_recv[1])
    for a in range(cycles):
        across = across + folded(r[a][0:8] * jnp.where(row[0:8] == 0, shell_recv[1, a : a + 1, :], 0.0))
    curvature = curvature - 2.0 * across

    dot_r[0, 0:8] = squares
    dot_r[0, 8:16] = curvature
    copies = [
        send(dot_r.at[0], dot_r.at[d], dotr_ss.at[d], dotr_rs.at[d], "radial", lax.rem(ri + d, nr))
        for d in range(1, nr)
    ]
    later += copies
    ker_copies = [
        send(ker_recv.at[0], ker_recv.at[d], ker_ss.at[d], ker_rs.at[d], "radial", lax.rem(ri + d, nr))
        for d in range(1, nr)
    ]
    later += ker_copies
    for name in ("pres", "therm", "table", "leg"):
        loads[name].wait()
    for copy in copies:
        copy.wait_recv()
    total = dot_r[0]
    for d in range(1, nr):
        total = total + dot_r[d]
    dot_l[0] = total
    copies = [
        send(dot_l.at[0], dot_l.at[d], dotl_ss.at[d], dotl_rs.at[d], "lateral", lax.rem(li + d, nl))
        for d in range(1, nl)
    ]
    later += copies
    for sender, receiver, ss, rs, axis, me, n in sides:
        @pl.when(me > 0)
        def _():
            edge(sender, receiver, ss, rs, 0, axis, lax.rem(me + n - 1, n)).start()

    for copy in copies:
        copy.wait_recv()
    total = dot_l[0]
    for d in range(1, nl):
        total = total + dot_l[d]
    alpha = jnp.sum(total[0:8], keepdims=True) / jnp.sum(total[8:16], keepdims=True)

    anomaly, pressure_new = [], []
    for a in range(cycles):
        new = pres[:, a, :] + alpha * r[a]
        pressure_new.append(new)
        anomaly.append((therm[:, a, :] - scale * new).astype(BF16))
    spectrum = jnp.dot(jnp.concatenate(anomaly, axis=0), table[...], preferred_element_type=F32).astype(BF16)
    for b in range(nr):
        for a in range(cycles):
            spec_send[b, :, a * block : (a + 1) * block] = spectrum[
                a * shells : (a + 1) * shells, b * block : (b + 1) * block
            ]
    copies = []
    for d in range(1, nr):
        target = lax.rem(ri + d, nr)
        copies.append(send(spec_send.at[target], spec_recv.at[d], spec_ss.at[d], spec_rs.at[d], "radial", target))
    later += copies
    spec_recv[0] = spec_send[ri]
    for copy in ker_copies:
        copy.wait_recv()
    for k in range(2):
        whole = jnp.concatenate([ker_recv[d, k].astype(F32) for d in range(nr)], axis=0)
        ker_t[k] = whole.T.astype(BF16)
    for copy in copies:
        copy.wait_recv()

    stack = jnp.concatenate([spec_recv[d] for d in range(nr)], axis=0)
    first = pl.multiple_of(lax.rem(ri * block, orders), block)
    sums = [[], []]
    for k in range(2):
        weighted = jnp.dot(ker_t[k], stack, preferred_element_type=F32)
        value = None
        for a in range(cycles):
            term = weighted[:, a * block : (a + 1) * block] * leg[a, :, pl.ds(first, block)].astype(F32)
            value = term if value is None else value + term
        for b in range(nl):
            piece = value[b * owned : (b + 1) * owned]
            part[k, b] = piece
            wire[k, b] = piece.astype(wire.dtype)
        for d in range(1, nl):
            target, slot = lax.rem(li + d, nl), k * nl + d
            sums[k].append(send(wire.at[k, target], terms.at[k, d], term_ss.at[slot], term_rs.at[slot], "lateral", target))
        later += sums[k]
    for sender, receiver, ss, rs, axis, me, n in sides:
        @pl.when(me < n - 1)
        def _():
            edge(sender, receiver, ss, rs, 0, axis, lax.rem(me + 1, n)).wait_recv()

        @pl.when(me == n - 1)
        def _():
            receiver[0] = jnp.zeros(receiver.shape[1:], F32)

    for a in range(cycles):
        image = inner[a] - jnp.where(row == shells - 1, shell_recv[0, a : a + 1, :], 0.0)
        image = image - jnp.where(row == 0, shell_recv[1, a : a + 1, :], 0.0)
        if a == 0:
            image = image - cycle_recv[1]
        if a == cycles - 1:
            image = image - cycle_recv[0]
        pres_out[:, a, :] = pressure_new[a]
        res_out[:, a, :] = r[a] - alpha * image
    stores = [
        pltpu.make_async_copy(pres_out, pres_hbm_out, store_sem.at[0]),
        pltpu.make_async_copy(res_out, res_hbm_out, store_sem.at[1]),
    ]
    for store in stores:
        store.start()
    mine = pl.ds(pl.multiple_of(ri * block, block), block)
    copies = []
    for k in range(2):
        total = part[k, li]
        for d in range(1, nl):
            sums[k][d - 1].wait_recv()
            total = total + terms[k, d].astype(F32)
        final[k, :, mine] = total
        for d in range(1, nr):
            here, slot = final.at[k, :, mine], k * nr + d
            copies.append(send(here, here, fin_ss.at[slot], fin_rs.at[slot], "radial", lax.rem(ri + d, nr)))
    for k in range(2):
        for d in range(1, nr):
            origin, slot = lax.rem(ri + nr - d, nr), k * nr + d
            theirs = pl.ds(pl.multiple_of(origin * block, block), block)
            pltpu.make_async_remote_copy(
                src_ref=final.at[k, :, theirs], dst_ref=final.at[k, :, theirs],
                send_sem=fin_ss.at[slot], recv_sem=fin_rs.at[slot],
                device_id={"radial": origin}, device_id_type=MESH,
            ).wait_recv()
    for c in range(2):
        geoid_out[:, c, :] = final[0, :, c * orders : (c + 1) * orders]
        topo_out[:, c, :] = final[1, :, c * orders : (c + 1) * orders]
    responses = [
        pltpu.make_async_copy(geoid_out, geoid_hbm_out, store_sem.at[2]),
        pltpu.make_async_copy(topo_out, topo_hbm_out, store_sem.at[3]),
    ]
    for store in responses:
        store.start()
    for copy in later + copies:
        copy.wait_send()
    for store in stores + responses:
        store.wait()
    for sender, receiver, ss, rs, axis, me, n in sides:
        @pl.when(me > 0)
        def _():
            edge(sender, receiver, ss, rs, 0, axis, lax.rem(me + n - 1, n)).wait_send()

        @pl.when(me < n - 1)
        def _():
            edge(sender, receiver, ss, rs, 1, axis, lax.rem(me + 1, n)).wait_send()


def placed(*refs):
    sources, targets, held, load_sem, store_sem = refs[:4], refs[4:8], refs[8:12], refs[12], refs[13]
    loads = [pltpu.make_async_copy(a, b, load_sem.at[i]) for i, (a, b) in enumerate(zip(sources, held))]
    stores = [pltpu.make_async_copy(a, b, store_sem.at[i]) for i, (a, b) in enumerate(zip(held, targets))]
    for load in loads:
        load.start()
    for load, store in zip(loads, stores):
        load.wait()
        store.start()
    for store in stores:
        store.wait()


def on_device(pressure, residual, inv_visc, thermal, compress, legendre, kernels):
    nr, nl = lax.axis_size("radial"), lax.axis_size("lateral")
    shells, cycles, nlon = residual.shape
    degrees, orders = legendre.shape[1:]
    owned = degrees // nl
    block = 2 * orders // nr
    wire = BF16 if owned % 16 == 0 else F32
    table = jnp.asarray(fourier_table(nlon, orders))
    dma = pltpu.SemaphoreType.DMA
    anywhere = pl.BlockSpec(memory_space=pl.ANY)
    operands = (pressure, residual, inv_visc, thermal, compress[None, :], legendre, kernels, table)
    outputs = (
        jax.ShapeDtypeStruct(pressure.shape, F32),
        jax.ShapeDtypeStruct(residual.shape, F32),
        jax.ShapeDtypeStruct((owned, 2, orders), F32),
        jax.ShapeDtypeStruct((owned, 2, orders), F32),
    )
    results = pl.pallas_call(
        functools.partial(kernel, nr, nl),
        out_shape=outputs,
        in_specs=[anywhere] * 8,
        out_specs=(anywhere,) * 4,
        scratch_shapes=[
            *(pltpu.VMEM(x.shape, x.dtype) for x in operands),
            dma((8,)),
            pltpu.VMEM((2, owned, 2 * orders), F32),
            *(pltpu.VMEM(x.shape, x.dtype) for x in outputs),
            dma((4,)),
            pltpu.VMEM((2, cycles, nlon), F32),
            pltpu.VMEM((2, cycles, nlon), F32),
            pltpu.VMEM((2, shells, nlon), F32),
            pltpu.VMEM((2, shells, nlon), F32),
            pltpu.VMEM((nr, 16, 128), F32),
            pltpu.VMEM((nl, 16, 128), F32),
            pltpu.VMEM((nr, shells, cycles * block), BF16),
            pltpu.VMEM((nr, shells, cycles * block), BF16),
            pltpu.VMEM((nr, 2, shells, degrees), BF16),
            pltpu.VMEM((2, degrees, nr * shells), BF16),
            pltpu.VMEM((2, nl, owned, block), F32),
            pltpu.VMEM((2, nl, owned, block), wire),
            pltpu.VMEM((2, nl, owned, block), wire),
            dma((2,)), dma((2,)), dma((2,)), dma((2,)),
            dma((nr,)), dma((nr,)), dma((nl,)), dma((nl,)),
            dma((nr,)), dma((nr,)), dma((nr,)), dma((nr,)),
            dma((2 * nl,)), dma((2 * nl,)), dma((2 * nr,)), dma((2 * nr,)),
        ],
        compiler_params=pltpu.CompilerParams(
            collective_id=0, has_side_effects=True, vmem_limit_bytes=60 * 2**20
        ),
    )(*operands)
    return pl.pallas_call(
        placed,
        out_shape=outputs,
        in_specs=[anywhere] * 4,
        out_specs=(anywhere,) * 4,
        scratch_shapes=[*(pltpu.VMEM(x.shape, x.dtype) for x in outputs), dma((4,)), dma((4,))],
        compiler_params=pltpu.CompilerParams(vmem_limit_bytes=60 * 2**20),
    )(*results)


def solution(mesh):
    return jax.shard_map(
        on_device,
        mesh=mesh,
        in_specs=(
            P("radial", "lateral", None),
            P("radial", "lateral", None),
            P("radial", "lateral", None),
            P("radial", "lateral", None),
            P("radial"),
            P("lateral", None, None),
            P(None, "radial", None),
        ),
        out_specs=(
            P("radial", "lateral", None),
            P("radial", "lateral", None),
            P("lateral", None, None),
            P("lateral", None, None),
        ),
        check_vma=False,
    )
```
